256 devices in a mesh: outer: 64 (over y_lo, z, x), inner: 4 (over y_hi, core).
Axes of the slice: x: 4, y: 4 (y_hi: 2, y_lo: 2; y = y_hi * 2 + y_lo), z: 8, core: 2. Of those that a mesh axis runs over, the one named last changes fastest.
Arguments:
- queries: bfloat16 [32768, 4096], P(('outer', 'inner')), may hold values from -10 to 10
- keys: bfloat16 [32768, 512], P(('outer', 'inner')), may hold values from -10 to 10
- values: bfloat16 [32768, 512], P(('outer', 'inner')), may hold values from -6 to 6
- grad_out: bfloat16 [32768, 4096], P(('outer', 'inner')), may hold values from -6 to 6
- stretch_order: int32 [256, 2], replicated, may hold values from 0 to 511, as said below
- block_keep: int32 [256, 3, 2, 2], replicated, may hold values 0 or 1
Outputs:
- grad_queries: bfloat16 [32768, 4096], P(('outer', 'inner'))
- grad_keys: bfloat16 [32768, 512], P(('outer', 'inner'))
- grad_values: bfloat16 [32768, 512], P(('outer', 'inner'))
The draws below stay inside these ranges and needn't reach their ends.
Inputs may be any that keep to these rules, and one draw needn't show every extreme that they name: `stretch_order`: each row holds two stretch numbers that add up to 511; over all rows every number of 0 to 511 appears once.
All inputs are finite; a program needn't handle non-finite values.
Results may differ from the reference program's by a relative error of at most 0.0084.
Values may be sent and summed in bfloat16 or wider, within the bound.
No kernel may reach another device: no remote copies, remote signals or barrier semaphores. Data moves between devices by JAX's collectives and lax.ppermute only.
A program may use at most 64 MiB of HBM per device.

```python
import jax
import jax.numpy as jnp
from jax import lax

HEADS = 32
KV_HEADS = 4
HEAD_DIM = 128
STRETCH = 64
HOLDERS = 256
TOKENS = 32768
N_OUTER = 64
N_INNER = 4


def draw_queries(key, part):
    key = jax.random.fold_in(key, 11)
    first = jax.random.fold_in(key, 0)
    shape = (TOKENS, KV_HEADS, HEADS // KV_HEADS, HEAD_DIM)
    result = jnp.clip(jax.random.normal(first, shape, jnp.float32), -6.0, 6.0)
    return result.reshape(TOKENS, HEADS * HEAD_DIM).astype(jnp.bfloat16)


def draw_keys(key, part):
    key = jax.random.fold_in(key, 12)
    first = jax.random.fold_in(key, 0)
    shape = (TOKENS, KV_HEADS, HEAD_DIM)
    result = jnp.clip(jax.random.normal(first, shape, jnp.float32), -6.0, 6.0)
    return result.reshape(TOKENS, KV_HEADS * HEAD_DIM).astype(jnp.bfloat16)


def draw_stretch_order(key, part):
    key = jax.random.fold_in(key, 13)
    order = jax.random.permutation(key, HOLDERS).astype(jnp.int32)
    return jnp.stack([order, 2 * HOLDERS - 1 - order], axis=1).astype(jnp.int32)


def touch_ends(array, rng, smallest, top_value):
    longest = array.shape.index(max(array.shape))
    spots = []
    for shift in (0, 1):
        where = [jax.random.randint(jax.random.fold_in(rng, axis), (), 0, length) for axis, length in enumerate(array.shape)]
        where[longest] = (where[longest] + shift) % array.shape[longest]
        spots.append(tuple(where))
    return array.at[spots[0]].set(smallest).at[spots[1]].set(top_value)


def levels(stream_key, shape, cuts, least, largest):
    level, own = 1.0, jax.random.fold_in(stream_key, 6)
    for axis_at, shards_of in cuts:
        steps = jnp.exp(jax.random.uniform(jax.random.fold_in(own, axis_at), (shards_of,), jnp.float32, least / len(cuts), largest / len(cuts)))
        level = level * jnp.repeat(steps, shape[axis_at] // shards_of).reshape([-1 if axis == axis_at else 1 for axis in range(len(shape))])
    return level


def gaussian(key, extent, spread, most, cuts=(), kind=jnp.bfloat16):
    gain = levels(key, extent, cuts, -0.22, 0.18) if cuts else 1.0
    drawn = jax.random.normal(key, extent, jnp.float32) * spread * gain
    return jnp.minimum(jnp.maximum(drawn, -most), most).astype(kind)


def setup_inputs(seed: int = 0) -> dict:
    key_of = jax.random.split(jax.random.key(seed), 7)
    queries = draw_queries(jax.random.fold_in(key_of[6], 71), 0)
    keys = draw_keys(jax.random.fold_in(key_of[6], 71), 0)
    values = gaussian(key_of[2], (TOKENS, KV_HEADS * HEAD_DIM), 1.0, 6.0, ((0, 256),))
    grad_out = gaussian(key_of[3], (TOKENS, HEADS * HEAD_DIM), 1.0, 6.0, ((0, 256),))
    stretch_order = draw_stretch_order(jax.random.fold_in(key_of[6], 71), 0)
    block_keep = touch_ends((jax.random.randint(key_of[5], (HOLDERS, 3, 2, 2), 0, 4) < 3).astype(jnp.int32), jax.random.fold_in(key_of[5], 1), 0, 1)
    return {"queries": queries, "keys": keys, "values": values, "grad_out": grad_out, "stretch_order": stretch_order, "block_keep": block_keep}


neg_big = -1.0e30


def reference(queries, keys, values, grad_out, stretch_order, block_keep):
    holders = N_OUTER * N_INNER
    group = HEADS // KV_HEADS
    scale = HEAD_DIM ** -0.5
    span = 2 * STRETCH
    query_blocks = queries.reshape(holders, span, KV_HEADS, group, HEAD_DIM)
    grad_blocks = grad_out.reshape(holders, span, KV_HEADS, group, HEAD_DIM)
    key_blocks = keys.reshape(holders, span, KV_HEADS, HEAD_DIM)
    value_blocks = values.reshape(holders, span, KV_HEADS, HEAD_DIM)
    grid = jnp.arange(holders, dtype=jnp.int32).reshape(N_OUTER, N_INNER)
    inner_prev = jnp.roll(grid, 1, axis=1).reshape(-1)
    outer_prev = jnp.roll(grid, 1, axis=0).reshape(-1)
    line = jnp.arange(STRETCH, dtype=jnp.int32)
    forced = jnp.zeros((3, 2, 2), jnp.int32).at[0, 0, 0].set(1).at[0, 1, 1].set(1)

    def one_holder(holder):
        sources = jnp.stack([holder, inner_prev[holder], outer_prev[holder]]).astype(jnp.int32)
        key_rows = key_blocks[sources].reshape(3 * span, KV_HEADS, HEAD_DIM).astype(jnp.float32)
        value_rows = value_blocks[sources].reshape(3 * span, KV_HEADS, HEAD_DIM).astype(jnp.float32)
        query_rows = query_blocks[holder].astype(jnp.float32)
        grad_rows = grad_blocks[holder].astype(jnp.float32)
        query_pos = (stretch_order[holder][:, None] * STRETCH + line[None, :]).reshape(-1)
        key_pos = (stretch_order[sources][:, :, None] * STRETCH + line[None, None, :]).reshape(-1)
        keep = jnp.maximum(block_keep[holder], forced)
        keep_wide = jnp.transpose(keep, (1, 0, 2)).reshape(2, 6)
        keep_full = jnp.repeat(jnp.repeat(keep_wide, STRETCH, axis=0), STRETCH, axis=1)
        allowed = (keep_full > 0) & (key_pos[None, :] <= query_pos[:, None])
        raw = jnp.einsum("qkgd,jkd->kgqj", query_rows, key_rows) * scale
        scores = jnp.where(allowed[None, None], raw, neg_big)
        peak = jnp.max(scores, axis=-1)
        total = jnp.sum(jnp.where(allowed[None, None], jnp.exp(scores - peak[..., None]), 0.0), axis=-1)
        log_norm = peak + jnp.log(total)
        probs = jnp.where(allowed[None, None], jnp.exp(scores - log_norm[..., None]), 0.0)
        probs_low = probs.astype(jnp.bfloat16).astype(jnp.float32)
        outputs = jnp.einsum("kgqj,jkd->qkgd", probs_low, value_rows)
        delta = jnp.transpose(jnp.sum(grad_rows * outputs, axis=-1), (1, 2, 0))
        grad_probs = jnp.einsum("qkgd,jkd->kgqj", grad_rows, value_rows)
        grad_scores = (probs * (grad_probs - delta[..., None]) * scale).astype(jnp.bfloat16).astype(jnp.float32)
        grad_query = jnp.einsum("kgqj,jkd->qkgd", grad_scores, key_rows)
        grad_key = jnp.einsum("kgqj,qkgd->jkd", grad_scores, query_rows)
        grad_value = jnp.einsum("kgqj,qkgd->jkd", probs_low, grad_rows)
        return (grad_query.reshape(span, HEADS * HEAD_DIM).astype(jnp.bfloat16),
                grad_key.reshape(3, span, KV_HEADS * HEAD_DIM),
                grad_value.reshape(3, span, KV_HEADS * HEAD_DIM))

    grad_query, key_parts, value_parts = lax.map(one_holder, jnp.arange(holders, dtype=jnp.int32))

    def collect(parts):
        parts = parts.reshape(N_OUTER, N_INNER, 3, span, KV_HEADS * HEAD_DIM)
        whole = parts[:, :, 0] + jnp.roll(parts[:, :, 1], -1, axis=1) + jnp.roll(parts[:, :, 2], -1, axis=0)
        return whole.reshape(TOKENS, KV_HEADS * HEAD_DIM).astype(jnp.bfloat16)

    return grad_query.reshape(TOKENS, HEADS * HEAD_DIM), collect(key_parts), collect(value_parts)
```

```python
import functools

import jax
import jax.numpy as jnp
from jax import lax
from jax.experimental import pallas as pl
from jax.experimental.pallas import tpu as pltpu
from jax.sharding import PartitionSpec as P

HEAD_DIM = 128
SCALE = HEAD_DIM ** -0.5
LOG2E = 1.4426950408889634
NEG_BIG = -1e30
VMEM = 16 * 1024 * 1024
NT = (((1,), (1,)), ((), ()))
NN = (((1,), (0,)), ((), ()))
TN = (((0,), (0,)), ((), ()))


def dot(a, b, dims):
    return lax.dot_general(a, b, dims, preferred_element_type=jnp.float32)


def from_behind(block, axis, distance):
    size = lax.axis_size(axis)
    return lax.ppermute(block, axis, [((i - distance) % size, i) for i in range(size)])


def head(ref, h, count=1):
    return ref[:, h * HEAD_DIM : (h + count) * HEAD_DIM]


def stack_heads(ref, first, count):
    return jnp.concatenate([head(ref, first + e) for e in range(count)], axis=0)


def stack_sources(refs, h):
    return jnp.concatenate([head(ref, h) for ref in refs], axis=0)


def fill_bias(meta, bias, stretch):
    lane = lax.broadcasted_iota(jnp.int32, (stretch, 2 * stretch), 1)
    line = lax.broadcasted_iota(jnp.int32, (stretch, 2 * stretch), 0)
    first = lane < stretch
    query_pos = jnp.where(first, meta[0] * stretch + lane, (meta[1] - 1) * stretch + lane)
    for s in range(3):
        for b in range(2):
            flags = [meta[6 + s * 4 + a * 2 + b] for a in range(2)]
            if s == 0:
                flags[b] = jnp.int32(1)
            flag = jnp.where(first, flags[0], flags[1])
            key_pos = meta[2 * s + b] * stretch + line
            allowed = (flag > 0) & (key_pos <= query_pos)
            row = (2 * s + b) * stretch
            bias[row : row + stretch, :] = jnp.where(allowed, 0.0, NEG_BIG)


def stage_kernel(meta, queries, grads, q, g, bias, sems):
    copies = [
        pltpu.make_async_copy(queries, q, sems.at[0]),
        pltpu.make_async_copy(grads, g, sems.at[1]),
    ]
    for copy in copies:
        copy.start()
    fill_bias(meta, bias, bias.shape[1] // 2)
    for copy in copies:
        copy.wait()


def probs_kernel(group, bias, q, g, ks, ki, ko, probs, dvs, dvi, dvo):
    span = q.shape[0]
    for h in range(ks.shape[1] // HEAD_DIM):
        lanes = slice(h * HEAD_DIM, (h + 1) * HEAD_DIM)
        keys = stack_sources((ks, ki, ko), h)
        for pair in range(group // 2):
            cols = slice(2 * pair * HEAD_DIM, (2 * pair + 2) * HEAD_DIM)
            query = stack_heads(q, h * group + 2 * pair, 2)
            wide = jnp.concatenate([bias[...], bias[...]], axis=1)
            scores = dot(keys, query, NT) * (SCALE * LOG2E) + wide
            peak = jnp.max(scores, axis=0, keepdims=True)
            raised = jnp.exp2(scores - peak)
            total = jnp.sum(raised, axis=0, keepdims=True)
            probs[h, :, cols] = (raised * (1.0 / total)).astype(jnp.bfloat16)
        out = dot(probs[h], stack_heads(g, h * group, group), NN)
        dvs[:, lanes] = out[:span]
        dvi[:, lanes] = out[span : 2 * span].astype(jnp.bfloat16)
        dvo[:, lanes] = out[2 * span :].astype(jnp.bfloat16)


def scores_kernel(group, q, g, vs, vi, vo, probs, dscores, dks, dki, dko):
    span = q.shape[0]
    for h in range(vs.shape[1] // HEAD_DIM):
        lanes = slice(h * HEAD_DIM, (h + 1) * HEAD_DIM)
        values = stack_sources((vs, vi, vo), h)
        for pair in range(group // 2):
            cols = slice(2 * pair * HEAD_DIM, (2 * pair + 2) * HEAD_DIM)
            grad_probs = dot(values, stack_heads(g, h * group + 2 * pair, 2), NT)
            weight = probs[h, :, cols].astype(jnp.float32)
            delta = jnp.sum(weight * grad_probs, axis=0, keepdims=True)
            dscores[h, :, cols] = (weight * ((grad_probs - delta) * SCALE)).astype(jnp.bfloat16)
        out = dot(dscores[h], stack_heads(q, h * group, group), NN)
        dks[:, lanes] = out[:span]
        dki[:, lanes] = out[span : 2 * span].astype(jnp.bfloat16)
        dko[:, lanes] = out[2 * span :].astype(jnp.bfloat16)


def queries_kernel(group, ks, ki, ko, dscores, dq):
    for h in range(ks.shape[1] // HEAD_DIM):
        keys = stack_sources((ks, ki, ko), h)
        for g in range(group):
            lanes = slice((h * group + g) * HEAD_DIM, (h * group + g + 1) * HEAD_DIM)
            cols = slice(g * HEAD_DIM, (g + 1) * HEAD_DIM)
            dq[:, lanes] = dot(dscores[h, :, cols], keys, TN).astype(jnp.bfloat16)


def add_kernel(a, b, c, d, e, f, dk, dv):
    dk[...] = (a[...] + b[...].astype(jnp.float32) + c[...].astype(jnp.float32)).astype(dk.dtype)
    dv[...] = (d[...] + e[...].astype(jnp.float32) + f[...].astype(jnp.float32)).astype(dv.dtype)


def shards(queries, keys, values, grad_out, stretch_order, block_keep):
    span = keys.shape[0]
    width = keys.shape[1]
    kv_heads = width // HEAD_DIM
    group = queries.shape[1] // width
    n_inner = lax.axis_size("inner")
    n_outer = lax.axis_size("outer")
    pos_outer = lax.axis_index("outer")
    pos_inner = lax.axis_index("inner")
    holder = pos_outer * n_inner + pos_inner
    inner_prev = pos_outer * n_inner + (pos_inner + n_inner - 1) % n_inner
    outer_prev = (pos_outer + n_outer - 1) % n_outer * n_inner + pos_inner
    k_out = from_behind(keys, "outer", 1)
    k_in = from_behind(keys, "inner", 1)
    v_out = from_behind(values, "outer", 1)
    v_in = from_behind(values, "inner", 1)
    orders = [lax.dynamic_index_in_dim(stretch_order, h, 0, False) for h in (holder, inner_prev, outer_prev)]
    keep = lax.dynamic_index_in_dim(block_keep, holder, 0, False).reshape(-1)
    meta = jnp.concatenate(orders + [keep])

    f32, bf16 = jnp.float32, jnp.bfloat16
    vmem = pl.BlockSpec(memory_space=pltpu.VMEM)
    smem = pl.BlockSpec(memory_space=pltpu.SMEM)
    hbm = pl.BlockSpec(memory_space=pl.ANY)
    rows = jax.ShapeDtypeStruct(queries.shape, bf16)
    table = jax.ShapeDtypeStruct((kv_heads, 3 * span, group * HEAD_DIM), bf16)
    kv32 = jax.ShapeDtypeStruct((span, width), f32)
    kv16 = jax.ShapeDtypeStruct((span, width), bf16)
    flops = 2 * span * queries.shape[1] * 3 * span

    def call(kernel, ins, out_shape, ops, scratch=()):
        return pl.pallas_call(
            kernel,
            in_specs=ins,
            out_specs=[vmem] * len(out_shape),
            out_shape=out_shape,
            scratch_shapes=scratch,
            compiler_params=pltpu.CompilerParams(vmem_limit_bytes=VMEM),
            cost_estimate=pl.CostEstimate(flops=ops * flops, bytes_accessed=2**20, transcendentals=0),
        )

    q, g, bias = call(
        stage_kernel,
        [smem, hbm, hbm],
        [rows, rows, jax.ShapeDtypeStruct((3 * span, span), f32)],
        1,
        [pltpu.SemaphoreType.DMA((2,))],
    )(meta, queries, grad_out)
    probs, dvs, dvi, dvo = call(
        functools.partial(probs_kernel, group), [vmem] * 6, [table, kv32, kv16, kv16], 2
    )(bias, q, g, keys, k_in, k_out)
    dv_out = from_behind(dvo, "outer", -1)
    dv_in = from_behind(dvi, "inner", -1)
    dscores, dks, dki, dko = call(
        functools.partial(scores_kernel, group), [vmem] * 6, [table, kv32, kv16, kv16], 2
    )(q, g, values, v_in, v_out, probs)
    dk_out = from_behind(dko, "outer", -1)
    dk_in = from_behind(dki, "inner", -1)
    (dq,) = call(functools.partial(queries_kernel, group), [vmem] * 4, [rows], 1)(keys, k_in, k_out, dscores)
    dk, dv = call(add_kernel, [vmem] * 6, [kv16, kv16], 0)(dks, dk_in, dk_out, dvs, dv_in, dv_out)
    return dq, dk, dv


def solution(mesh):
    rows = P(("outer", "inner"), None)
    return jax.shard_map(
        shards, mesh=mesh, in_specs=(rows, rows, rows, rows, P(), P()), out_specs=(rows, rows, rows), check_vma=False
    )
```

```python
import functools

import jax
import jax.numpy as jnp
from jax import lax
from jax.experimental import pallas as pl
from jax.experimental.pallas import tpu as pltpu
from jax.sharding import PartitionSpec as P

HEAD_DIM = 128
SCALE = HEAD_DIM ** -0.5
LOG2E = 1.4426950408889634
NEG_BIG = -1e30
VMEM = 16 * 1024 * 1024
NT = (((1,), (1,)), ((), ()))
NN = (((1,), (0,)), ((), ()))
TN = (((0,), (0,)), ((), ()))


def dot(a, b, dims):
    return lax.dot_general(a, b, dims, preferred_element_type=jnp.float32)


def from_behind(block, axis, distance):
    size = lax.axis_size(axis)
    return lax.ppermute(block, axis, [((i - distance) % size, i) for i in range(size)])


def head(ref, h, count=1):
    return ref[:, h * HEAD_DIM : (h + count) * HEAD_DIM]


def stack_heads(ref, first, count):
    return jnp.concatenate([head(ref, first + e) for e in range(count)], axis=0)


def stack_sources(refs, h):
    return jnp.concatenate([head(ref, h) for ref in refs], axis=0)


def fill_bias(meta, bias, stretch):
    lane = lax.broadcasted_iota(jnp.int32, (stretch, 2 * stretch), 1)
    line = lax.broadcasted_iota(jnp.int32, (stretch, 2 * stretch), 0)
    first = lane < stretch
    query_pos = jnp.where(first, meta[0] * stretch + lane, (meta[1] - 1) * stretch + lane)
    for s in range(3):
        for b in range(2):
            flags = [meta[6 + s * 4 + a * 2 + b] for a in range(2)]
            if s == 0:
                flags[b] = jnp.int32(1)
            flag = jnp.where(first, flags[0], flags[1])
            key_pos = meta[2 * s + b] * stretch + line
            allowed = (flag > 0) & (key_pos <= query_pos)
            row = (2 * s + b) * stretch
            bias[row : row + stretch, :] = jnp.where(allowed, 0.0, NEG_BIG)


def stage_kernel(queries, grads, keys, values, q, g, k, v, sems):
    copies = [
        pltpu.make_async_copy(source, target, sems.at[n])
        for n, (source, target) in enumerate(((queries, q), (grads, g), (keys, k), (values, v)))
    ]
    for copy in copies:
        copy.start()
    for copy in copies:
        copy.wait()


def bias_kernel(meta, bias):
    fill_bias(meta, bias, bias.shape[1] // 2)


def probs_kernel(group, bias, q, g, ks, ki, ko, probs, dvs, dvi, dvo, work):
    span = q.shape[0]
    outs = []
    for h in range(ks.shape[1] // HEAD_DIM):
        keys = stack_sources((ks, ki, ko), h)
        for pair in range(group // 2):
            cols = slice(2 * pair * HEAD_DIM, (2 * pair + 2) * HEAD_DIM)
            query = stack_heads(q, h * group + 2 * pair, 2)
            wide = jnp.concatenate([bias[...], bias[...]], axis=1)
            scores = dot(keys, query, NT) * (SCALE * LOG2E) + wide
            peak = jnp.max(scores, axis=0, keepdims=True)
            raised = jnp.exp2(scores - peak)
            total = jnp.sum(raised, axis=0, keepdims=True)
            work[h, :, cols] = (raised * (1.0 / total)).astype(jnp.bfloat16)
        outs.append(dot(work[h], stack_heads(g, h * group, group), NN))
    for h, out in enumerate(outs):
        lanes = slice(h * HEAD_DIM, (h + 1) * HEAD_DIM)
        dvs[:, lanes] = out[:span]
        dvi[:, lanes] = out[span : 2 * span].astype(jnp.bfloat16)
        dvo[:, lanes] = out[2 * span :].astype(jnp.bfloat16)
    probs[...] = work[...]


def scores_kernel(group, q, g, vs, vi, vo, probs, dscores, dks, dki, dko, work):
    span = q.shape[0]
    outs = []
    for h in range(vs.shape[1] // HEAD_DIM):
        values = stack_sources((vs, vi, vo), h)
        for pair in range(group // 2):
            cols = slice(2 * pair * HEAD_DIM, (2 * pair + 2) * HEAD_DIM)
            grad_probs = dot(values, stack_heads(g, h * group + 2 * pair, 2), NT)
            weight = probs[h, :, cols].astype(jnp.float32)
            delta = jnp.sum(weight * grad_probs, axis=0, keepdims=True)
            work[h, :, cols] = (weight * ((grad_probs - delta) * SCALE)).astype(jnp.bfloat16)
        outs.append(dot(work[h], stack_heads(q, h * group, group), NN))
    for h, out in enumerate(outs):
        lanes = slice(h * HEAD_DIM, (h + 1) * HEAD_DIM)
        dks[:, lanes] = out[:span]
        dki[:, lanes] = out[span : 2 * span].astype(jnp.bfloat16)
        dko[:, lanes] = out[2 * span :].astype(jnp.bfloat16)
    dscores[...] = work[...]


def queries_kernel(group, ks, ki, ko, dscores, dvs, dvi, dvo, dq, dv):
    dv[...] = (dvs[...] + dvi[...].astype(jnp.float32) + dvo[...].astype(jnp.float32)).astype(dv.dtype)
    outs = []
    for h in range(ks.shape[1] // HEAD_DIM):
        keys = stack_sources((ks, ki, ko), h)
        outs.append(dot(keys, dscores[h], TN).astype(jnp.bfloat16))
    for h, out in enumerate(outs):
        for g in range(group):
            lanes = slice((h * group + g) * HEAD_DIM, (h * group + g + 1) * HEAD_DIM)
            dq[:, lanes] = out[:, g * HEAD_DIM : (g + 1) * HEAD_DIM].T


def add_kernel(a, b, c, out):
    out[...] = (a[...] + b[...].astype(jnp.float32) + c[...].astype(jnp.float32)).astype(out.dtype)


def shards(queries, keys, values, grad_out, stretch_order, block_keep):
    span = keys.shape[0]
    width = keys.shape[1]
    kv_heads = width // HEAD_DIM
    group = queries.shape[1] // width
    n_inner = lax.axis_size("inner")
    n_outer = lax.axis_size("outer")
    pos_outer = lax.axis_index("outer")
    pos_inner = lax.axis_index("inner")
    holder = pos_outer * n_inner + pos_inner
    inner_prev = pos_outer * n_inner + (pos_inner + n_inner - 1) % n_inner
    outer_prev = (pos_outer + n_outer - 1) % n_outer * n_inner + pos_inner
    k_out = from_behind(keys, "outer", 1)
    k_in = from_behind(keys, "inner", 1)
    orders = [lax.dynamic_index_in_dim(stretch_order, h, 0, False) for h in (holder, inner_prev, outer_prev)]
    keep = lax.dynamic_index_in_dim(block_keep, holder, 0, False).reshape(-1)
    meta = jnp.concatenate(orders + [keep])

    f32, bf16 = jnp.float32, jnp.bfloat16
    vmem = pl.BlockSpec(memory_space=pltpu.VMEM)
    smem = pl.BlockSpec(memory_space=pltpu.SMEM)
    hbm = pl.BlockSpec(memory_space=pltpu.HBM)
    rows = jax.ShapeDtypeStruct(queries.shape, bf16)
    table = jax.ShapeDtypeStruct((kv_heads, 3 * span, group * HEAD_DIM), bf16)
    kv32 = jax.ShapeDtypeStruct((span, width), f32)
    kv16 = jax.ShapeDtypeStruct((span, width), bf16)
    flops = 2 * span * queries.shape[1] * 3 * span

    def call(kernel, ins, out_shape, ops, scratch=(), size=2**20):
        return pl.pallas_call(
            kernel,
            in_specs=ins,
            out_specs=[vmem] * len(out_shape),
            out_shape=out_shape,
            scratch_shapes=scratch,
            compiler_params=pltpu.CompilerParams(vmem_limit_bytes=VMEM),
            cost_estimate=pl.CostEstimate(flops=ops * flops, bytes_accessed=size, transcendentals=0),
        )

    q, g, k, v = call(stage_kernel, [hbm] * 4, [rows, rows, kv16, kv16], 0, [pltpu.SemaphoreType.DMA((4,))])(
        *(pltpu.with_memory_space_constraint(x, pltpu.HBM) for x in (queries, grad_out, keys, values))
    )
    v_out = from_behind(values, "outer", 1)
    v_in = from_behind(values, "inner", 1)
    (bias,) = call(bias_kernel, [smem], [jax.ShapeDtypeStruct((3 * span, span), f32)], 0)(meta)
    work = [pltpu.VMEM(table.shape, bf16)]
    probs, dvs, dvi, dvo = call(
        functools.partial(probs_kernel, group), [vmem] * 6, [table, kv32, kv16, kv16], 2, work
    )(bias, q, g, k, k_in, k_out)
    dv_out = from_behind(dvo, "outer", -1)
    dv_in = from_behind(dvi, "inner", -1)
    dscores, dks, dki, dko = call(
        functools.partial(scores_kernel, group), [vmem] * 6, [table, kv32, kv16, kv16], 2, work
    )(q, g, v, v_in, v_out, probs)
    dk_out = from_behind(dko, "outer", -1)
    dk_in = from_behind(dki, "inner", -1)
    dq, dv = call(functools.partial(queries_kernel, group), [vmem] * 7, [rows, kv16], 1)(
        k, k_in, k_out, dscores, dvs, dv_in, dv_out
    )
    dks, dq, dv = lax.optimization_barrier((dks, dq, dv))
    (dk,) = call(add_kernel, [vmem] * 3, [kv16], 0)(dks, dk_in, dk_out)
    return dq, dk, dv


def solution(mesh):
    rows = P(("outer", "inner"), None)
    return jax.shard_map(
        shards, mesh=mesh, in_specs=(rows, rows, rows, rows, P(), P()), out_specs=(rows, rows, rows), check_vma=False
    )
```

```python
import functools

import jax
import jax.numpy as jnp
from jax import lax
from jax.experimental import pallas as pl
from jax.experimental.pallas import tpu as pltpu
from jax.sharding import PartitionSpec as P

HEAD_DIM = 128
SCALE = HEAD_DIM ** -0.5
LOG2E = 1.4426950408889634
NEG_BIG = -1e30
VMEM = 16 * 1024 * 1024
NT = (((1,), (1,)), ((), ()))
NN = (((1,), (0,)), ((), ()))
TN = (((0,), (0,)), ((), ()))


def dot(a, b, dims):
    return lax.dot_general(a, b, dims, preferred_element_type=jnp.float32)


def ring(block, axis, step):
    size = lax.axis_size(axis)
    return lax.ppermute(block, axis, [(i, (i + step) % size) for i in range(size)])


def head(ref, h, count=1):
    return ref[:, h * HEAD_DIM : (h + count) * HEAD_DIM]


def stack_heads(ref, first, count):
    return jnp.concatenate([head(ref, first + e) for e in range(count)], axis=0)


def stack_sources(refs, h):
    return jnp.concatenate([head(ref, h) for ref in refs], axis=0)


def fill_bias(holder, inner_prev, outer_prev, order, keep, bias):
    stretch = bias.shape[1] // 2
    lane = lax.broadcasted_iota(jnp.int32, (stretch, 2 * stretch), 1)
    line = lax.broadcasted_iota(jnp.int32, (stretch, 2 * stretch), 0)
    place = lax.broadcasted_iota(jnp.int32, order.shape, 1)
    first = lane < stretch

    def pick(table, column):
        return jnp.sum(jnp.where(place == column, table, 0), axis=1, keepdims=True)

    numbers = [pick(order[...], column) for column in (holder, inner_prev, outer_prev)]
    own = numbers[0]
    query_pos = jnp.where(first, own[0:1] * stretch + lane, (own[1:2] - 1) * stretch + lane)
    for s in range(3):
        flags = [pick(keep[s, a], holder) for a in range(2)]
        for b in range(2):
            flag = jnp.where(first, flags[0][b : b + 1], flags[1][b : b + 1])
            if s == 0:
                flag = jnp.where(first if b == 0 else ~first, 1, flag)
            key_pos = numbers[s][b : b + 1] * stretch + line
            allowed = (flag > 0) & (key_pos <= query_pos)
            row = (2 * s + b) * stretch
            bias[row : row + stretch, :] = jnp.where(allowed, 0.0, NEG_BIG)


def stage_kernel(orders, keeps, queries, grads, keys, values, q, g, k, v, bias, order, keep, sems):
    moves = ((orders, order), (keeps, keep), (values, v), (keys, k), (queries, q), (grads, g))
    copies = [pltpu.make_async_copy(*move, sems.at[n]) for n, move in enumerate(moves)]
    for copy in copies:
        copy.start()
    for copy in copies[:2]:
        copy.wait()
    n_inner, n_outer = lax.axis_size("inner"), lax.axis_size("outer")
    pos_inner, pos_outer = lax.axis_index("inner"), lax.axis_index("outer")
    inner_prev = lax.rem(pos_inner + n_inner - 1, n_inner)
    outer_prev = lax.rem(pos_outer + n_outer - 1, n_outer)
    fill_bias(
        pos_outer * n_inner + pos_inner,
        pos_outer * n_inner + inner_prev,
        outer_prev * n_inner + pos_inner,
        order,
        keep,
        bias,
    )
    for copy in copies[2:]:
        copy.wait()


def pairs(group, kv_heads):
    for h in range(kv_heads):
        for pair in range(group // 2):
            yield h, h * group + 2 * pair, slice(2 * pair * HEAD_DIM, (2 * pair + 2) * HEAD_DIM)


def masked_scores(keys, query, bias):
    return dot(keys, query, NT) * (SCALE * LOG2E) + jnp.concatenate([bias, bias], axis=1)


def own_kernel(group, bias, q, g, k, v, raised, grad_probs, stats):
    span = q.shape[0]
    for h, first, cols in pairs(group, k.shape[1] // HEAD_DIM):
        scores = masked_scores(head(k, h), stack_heads(q, first, 2), bias[:span])
        peak = jnp.max(scores, axis=0, keepdims=True)
        weight = jnp.exp2(scores - peak)
        grads = dot(head(v, h), stack_heads(g, first, 2), NT)
        raised[h, :, cols] = weight.astype(jnp.bfloat16)
        grad_probs[h, :, cols] = grads
        stats[h, 0:1, cols] = peak
        stats[h, 1:2, cols] = jnp.sum(weight, axis=0, keepdims=True)
        stats[h, 2:3, cols] = jnp.sum(weight * grads, axis=0, keepdims=True)


def write_terms(outs, outer, inner):
    span = inner.shape[0]
    for h, out in enumerate(outs):
        lanes = slice(h * HEAD_DIM, (h + 1) * HEAD_DIM)
        inner[:, lanes] = out[:span].astype(inner.dtype)
        outer[:, lanes] = out[span:].astype(outer.dtype)


def probs_kernel(group, bias, q, g, ki, ko, stats, probs, rows, outer, inner, work):
    span = q.shape[0]
    outs = []
    for h, first, cols in pairs(group, ki.shape[1] // HEAD_DIM):
        if first == h * group:
            keys = stack_sources((ki, ko), h)
        scores = masked_scores(keys, stack_heads(q, first, 2), bias[span:])
        own_peak = stats[h, 0:1, cols]
        peak = jnp.maximum(own_peak, jnp.max(scores, axis=0, keepdims=True))
        raised = jnp.exp2(scores - peak)
        lowered = jnp.exp2(own_peak - peak)
        scale = 1.0 / (jnp.sum(raised, axis=0, keepdims=True) + lowered * stats[h, 1:2, cols])
        work[h, :, cols] = (raised * scale).astype(jnp.bfloat16)
        rows[h, 0:1, cols] = lowered * scale
        rows[h, 1:2, cols] = lowered * scale * stats[h, 2:3, cols]
        if first == (h + 1) * group - 2:
            outs.append(dot(work[h], stack_heads(g, h * group, group), NN))
    write_terms(outs, outer, inner)
    probs[...] = work[...]


def scores_kernel(group, q, g, vi, vo, probs, rows, dscores, deltas, outer, inner, work):
    outs = []
    for h, first, cols in pairs(group, vi.shape[1] // HEAD_DIM):
        if first == h * group:
            values = stack_sources((vi, vo), h)
        grad_probs = dot(values, stack_heads(g, first, 2), NT)
        weight = probs[h, :, cols].astype(jnp.float32)
        delta = rows[h, 1:2, cols] + jnp.sum(weight * grad_probs, axis=0, keepdims=True)
        work[h, :, cols] = (weight * (grad_probs - delta)).astype(jnp.bfloat16)
        deltas[h, 0:1, cols] = delta
        if first == (h + 1) * group - 2:
            outs.append(dot(work[h], stack_heads(q, h * group, group), NN) * SCALE)
    write_terms(outs, outer, inner)
    dscores[...] = work[...]


def queries_kernel(
    group, q, g, ks, ki, ko, raised, grad_probs, rows, deltas, dscores, dvi, dvo, dq, dk, dv, own_probs, own_scores
):
    f32, bf16 = jnp.float32, jnp.bfloat16
    kv_heads = ks.shape[1] // HEAD_DIM
    for h, first, cols in pairs(group, kv_heads):
        weight = raised[h, :, cols].astype(f32) * rows[h, 0:1, cols]
        own_probs[h, :, cols] = weight.astype(bf16)
        own_scores[h, :, cols] = (weight * (grad_probs[h, :, cols] - deltas[h, 0:1, cols])).astype(bf16)
    outs = []
    for h in range(kv_heads):
        lanes = slice(h * HEAD_DIM, (h + 1) * HEAD_DIM)
        terms = dvi[:, lanes].astype(f32) + dvo[:, lanes].astype(f32)
        dv[:, lanes] = (dot(own_probs[h], stack_heads(g, h * group, group), NN) + terms).astype(bf16)
        dk[:, lanes] = dot(own_scores[h], stack_heads(q, h * group, group), NN) * SCALE
        wide = jnp.concatenate([own_scores[h], dscores[h]], axis=0)
        outs.append((dot(stack_sources((ks, ki, ko), h), wide, TN) * SCALE).astype(bf16))
    for h, out in enumerate(outs):
        for e in range(group):
            lanes = slice((h * group + e) * HEAD_DIM, (h * group + e + 1) * HEAD_DIM)
            dq[:, lanes] = out[:, e * HEAD_DIM : (e + 1) * HEAD_DIM].T


def gate_kernel(x, vi, vo, out):
    out[...] = x[...]


def add_kernel(a, b, c, out):
    out[...] = (a[...] + b[...].astype(jnp.float32) + c[...].astype(jnp.float32)).astype(out.dtype)


def shards(queries, keys, values, grad_out, stretch_order, block_keep):
    span = keys.shape[0]
    width = keys.shape[1]
    kv_heads = width // HEAD_DIM
    group = queries.shape[1] // width

    f32, bf16 = jnp.float32, jnp.bfloat16
    vmem = pl.BlockSpec(memory_space=pltpu.VMEM)
    hbm = pl.BlockSpec(memory_space=pltpu.HBM)
    rows = jax.ShapeDtypeStruct(queries.shape, bf16)
    wide = group * HEAD_DIM
    away = jax.ShapeDtypeStruct((kv_heads, 2 * span, wide), bf16)
    own16 = jax.ShapeDtypeStruct((kv_heads, span, wide), bf16)
    own32 = jax.ShapeDtypeStruct((kv_heads, span, wide), f32)
    stat = jax.ShapeDtypeStruct((kv_heads, 8, wide), f32)
    kv32 = jax.ShapeDtypeStruct((span, width), f32)
    kv16 = jax.ShapeDtypeStruct((span, width), bf16)
    work = [pltpu.VMEM(away.shape, bf16)]

    def call(kernel, ins, out_shape, scratch=()):
        return pl.pallas_call(
            kernel,
            in_specs=ins,
            out_specs=[vmem] * len(out_shape),
            out_shape=out_shape,
            scratch_shapes=scratch,
            compiler_params=pltpu.CompilerParams(vmem_limit_bytes=VMEM),
            cost_estimate=pl.CostEstimate(flops=1, bytes_accessed=1, transcendentals=0),
        )

    def run(kernel, ins, out_shape, scratch=()):
        return call(functools.partial(kernel, group), [vmem] * len(ins), out_shape, scratch)(*ins)

    k_out = ring(keys, "outer", 1)
    k_in = ring(keys, "inner", 1)
    tables = stretch_order.T, block_keep.transpose(1, 2, 3, 0)
    q, g, k, v, bias = call(
        stage_kernel,
        [hbm] * 6,
        [rows, rows, kv16, kv16, jax.ShapeDtypeStruct((3 * span, span), f32)],
        [pltpu.VMEM(x.shape, x.dtype) for x in tables] + [pltpu.SemaphoreType.DMA((6,))],
    )(*(pltpu.with_memory_space_constraint(x, pltpu.HBM) for x in (*tables, queries, grad_out, keys, values)))
    v_out = ring(v, "outer", 1)
    v_in = ring(v, "inner", 1)
    raised, grad_probs, stats = run(own_kernel, (bias, q, g, k, v), [own16, own32, stat])
    probs, row_scale, dvo, dvi = run(
        probs_kernel, (bias, q, g, k_in, k_out, stats), [away, stat, kv16, kv16], work
    )
    dv_in = ring(dvi, "inner", -1)
    (dvo,) = call(gate_kernel, [vmem] * 3, [kv16])(dvo, v_in, v_out)
    dv_out = ring(dvo, "outer", -1)
    dscores, deltas, dko, dki = run(
        scores_kernel, (q, g, v_in, v_out, probs, row_scale), [away, stat, kv16, kv16], work
    )
    dk_in = ring(dki, "inner", -1)
    dk_out = ring(dko, "outer", -1)
    dq, dks, dv = run(
        queries_kernel,
        (q, g, k, k_in, k_out, raised, grad_probs, row_scale, deltas, dscores, dv_in, dv_out),
        [rows, kv32, kv16],
        [pltpu.VMEM(own16.shape, bf16)] * 2,
    )
    (dk,) = call(add_kernel, [vmem] * 3, [kv16])(dks, dk_in, dk_out)
    return dq, dk, dv


def solution(mesh):
    rows = P(("outer", "inner"), None)
    return jax.shard_map(
        shards, mesh=mesh, in_specs=(rows, rows, rows, rows, P(), P()), out_specs=(rows, rows, rows), check_vma=False
    )
```

```python
import functools

import jax
import jax.numpy as jnp
from jax import lax
from jax.experimental import pallas as pl
from jax.experimental.pallas import tpu as pltpu
from jax.sharding import PartitionSpec as P

HEAD_DIM = 128
SCALE = HEAD_DIM ** -0.5
LOG2E = 1.4426950408889634
NEG_BIG = -1e30
VMEM = 16 * 1024 * 1024
NT = (((1,), (1,)), ((), ()))
NN = (((1,), (0,)), ((), ()))
TN = (((0,), (0,)), ((), ()))


def dot(a, b, dims):
    return lax.dot_general(a, b, dims, preferred_element_type=jnp.float32)


def ring(block, axis, step):
    size = lax.axis_size(axis)
    return lax.ppermute(block, axis, [(i, (i + step) % size) for i in range(size)])


def head(ref, h, count=1):
    return ref[:, h * HEAD_DIM : (h + count) * HEAD_DIM]


def stack_heads(ref, first, count):
    return jnp.concatenate([head(ref, first + e) for e in range(count)], axis=0)


def stack_sources(refs, h):
    return jnp.concatenate([head(ref, h) for ref in refs], axis=0)


def fill_bias(holder, inner_prev, outer_prev, order, keep, bias):
    stretch = bias.shape[1] // 2
    lane = lax.broadcasted_iota(jnp.int32, (stretch, 2 * stretch), 1)
    line = lax.broadcasted_iota(jnp.int32, (stretch, 2 * stretch), 0)
    place = lax.broadcasted_iota(jnp.int32, order.shape, 1)
    first = lane < stretch

    def pick(table, column):
        return jnp.sum(jnp.where(place == column, table, 0), axis=1, keepdims=True)

    numbers = [pick(order[...], column) for column in (holder, inner_prev, outer_prev)]
    own = numbers[0]
    query_pos = jnp.where(first, own[0:1] * stretch + lane, (own[1:2] - 1) * stretch + lane)
    for s in range(3):
        flags = [pick(keep[s, a], holder) for a in range(2)]
        for b in range(2):
            flag = jnp.where(first, flags[0][b : b + 1], flags[1][b : b + 1])
            if s == 0:
                flag = jnp.where(first if b == 0 else ~first, 1, flag)
            key_pos = numbers[s][b : b + 1] * stretch + line
            allowed = (flag > 0) & (key_pos <= query_pos)
            row = (2 * s + b) * stretch
            bias[row : row + stretch, :] = jnp.where(allowed, 0.0, NEG_BIG)


def stage_kernel(orders, keeps, queries, grads, keys, values, q, g, k, v, bias, order, keep, sems):
    moves = ((orders, order), (keeps, keep), (values, v), (keys, k), (queries, q), (grads, g))
    copies = [pltpu.make_async_copy(*move, sems.at[n]) for n, move in enumerate(moves)]
    for copy in copies:
        copy.start()
    for copy in copies[:2]:
        copy.wait()
    n_inner, n_outer = lax.axis_size("inner"), lax.axis_size("outer")
    pos_inner, pos_outer = lax.axis_index("inner"), lax.axis_index("outer")
    inner_prev = lax.rem(pos_inner + n_inner - 1, n_inner)
    outer_prev = lax.rem(pos_outer + n_outer - 1, n_outer)
    fill_bias(
        pos_outer * n_inner + pos_inner,
        pos_outer * n_inner + inner_prev,
        outer_prev * n_inner + pos_inner,
        order,
        keep,
        bias,
    )
    for copy in copies[2:]:
        copy.wait()


def pairs(group, kv_heads):
    for h in range(kv_heads):
        for pair in range(group // 2):
            yield h, h * group + 2 * pair, slice(2 * pair * HEAD_DIM, (2 * pair + 2) * HEAD_DIM)


def masked_scores(keys, query, bias):
    return dot(keys, query, NT) * (SCALE * LOG2E) + jnp.concatenate([bias, bias], axis=1)


def own_kernel(group, bias, q, g, k, v, raised, grad_probs, stats):
    span = q.shape[0]
    for h, first, cols in pairs(group, k.shape[1] // HEAD_DIM):
        scores = masked_scores(head(k, h), stack_heads(q, first, 2), bias[:span])
        peak = jnp.max(scores, axis=0, keepdims=True)
        weight = jnp.exp2(scores - peak)
        grads = dot(head(v, h), stack_heads(g, first, 2), NT)
        raised[h, :, cols] = weight.astype(jnp.bfloat16)
        grad_probs[h, :, cols] = grads
        stats[h, 0:1, cols] = peak
        stats[h, 1:2, cols] = jnp.sum(weight, axis=0, keepdims=True)
        stats[h, 2:3, cols] = jnp.sum(weight * grads, axis=0, keepdims=True)


def write_terms(outs, outer, inner):
    span = inner.shape[0]
    for h, out in enumerate(outs):
        lanes = slice(h * HEAD_DIM, (h + 1) * HEAD_DIM)
        inner[:, lanes] = out[:span].astype(inner.dtype)
        outer[:, lanes] = out[span:].astype(outer.dtype)


def by_pairs(group, kv_heads, product, finish, gather):
    steps = list(pairs(group, kv_heads))
    outs = []
    ahead = product(*steps[0])
    for n, step in enumerate(steps):
        block = ahead
        if n + 1 < len(steps):
            ahead = product(*steps[n + 1])
        h, first, cols = step
        if gather and h > 0 and first == h * group + 2:
            outs.append(gather(h - 1))
        finish(h, cols, block)
    if gather:
        outs.append(gather(kv_heads - 1))
    return outs


def outer_kernel(group, bias, q, ko, raised, stats, work, rows):
    span = q.shape[0]

    def finish(h, cols, products):
        scores = products * (SCALE * LOG2E) + jnp.concatenate([bias[2 * span :]] * 2, axis=1)
        peak = jnp.max(scores, axis=0, keepdims=True)
        weight = jnp.exp2(scores - peak)
        work[h, :, cols] = weight.astype(jnp.bfloat16)
        rows[h, 0:1, cols] = peak
        rows[h, 1:2, cols] = jnp.sum(weight, axis=0, keepdims=True)

    by_pairs(
        group,
        ko.shape[1] // HEAD_DIM,
        lambda h, first, cols: dot(head(ko, h), stack_heads(q, first, 2), NT),
        finish,
        None,
    )
    raised[...] = work[...]
    stats[...] = rows[...]


def probs_kernel(group, bias, q, g, ki, stats, raised, outer_stats, probs, rows_out, outer, inner, work, rows):
    span = q.shape[0]

    def finish(h, cols, products):
        scores = products * (SCALE * LOG2E) + jnp.concatenate([bias[span : 2 * span]] * 2, axis=1)
        own_peak, outer_peak = stats[h, 0:1, cols], outer_stats[h, 0:1, cols]
        peak = jnp.maximum(jnp.maximum(own_peak, outer_peak), jnp.max(scores, axis=0, keepdims=True))
        weight = jnp.exp2(scores - peak)
        lowered, far = jnp.exp2(own_peak - peak), jnp.exp2(outer_peak - peak)
        total = jnp.sum(weight, axis=0, keepdims=True) + lowered * stats[h, 1:2, cols]
        scale = 1.0 / (total + far * outer_stats[h, 1:2, cols])
        work[h, :span, cols] = (weight * scale).astype(jnp.bfloat16)
        work[h, span:, cols] = (raised[h, :, cols].astype(jnp.float32) * (far * scale)).astype(jnp.bfloat16)
        rows[h, 0:1, cols] = lowered * scale
        rows[h, 1:2, cols] = lowered * scale * stats[h, 2:3, cols]

    outs = by_pairs(
        group,
        ki.shape[1] // HEAD_DIM,
        lambda h, first, cols: dot(head(ki, h), stack_heads(q, first, 2), NT),
        finish,
        lambda h: dot(work[h], stack_heads(g, h * group, group), NN),
    )
    write_terms(outs, outer, inner)
    probs[...] = work[...]
    rows_out[...] = rows[...]


def scores_kernel(group, q, g, vi, vo, probs, rows, dscores, deltas_out, outer, inner, work, deltas):
    values = [stack_sources((vi, vo), h) for h in range(vi.shape[1] // HEAD_DIM)]

    def finish(h, cols, grad_probs):
        weight = probs[h, :, cols].astype(jnp.float32)
        delta = rows[h, 1:2, cols] + jnp.sum(weight * grad_probs, axis=0, keepdims=True)
        work[h, :, cols] = (weight * (grad_probs - delta)).astype(jnp.bfloat16)
        deltas[h, 0:1, cols] = delta

    outs = by_pairs(
        group,
        len(values),
        lambda h, first, cols: dot(values[h], stack_heads(g, first, 2), NT),
        finish,
        lambda h: dot(work[h], stack_heads(q, h * group, group), NN) * SCALE,
    )
    write_terms(outs, outer, inner)
    dscores[...] = work[...]
    deltas_out[...] = deltas[...]


def queries_kernel(
    group, q, g, ks, ki, ko, raised, grad_probs, rows, deltas, dscores, dq, dk, dv, own_probs, own_scores
):
    f32, bf16 = jnp.float32, jnp.bfloat16
    kv_heads = ks.shape[1] // HEAD_DIM
    for h, first, cols in pairs(group, kv_heads):
        weight = raised[h, :, cols].astype(f32) * rows[h, 0:1, cols]
        own_probs[h, :, cols] = weight.astype(bf16)
        own_scores[h, :, cols] = (weight * (grad_probs[h, :, cols] - deltas[h, 0:1, cols])).astype(bf16)
    outs = []
    for h in range(kv_heads):
        lanes = slice(h * HEAD_DIM, (h + 1) * HEAD_DIM)
        dv[:, lanes] = dot(own_probs[h], stack_heads(g, h * group, group), NN)
        dk[:, lanes] = dot(own_scores[h], stack_heads(q, h * group, group), NN) * SCALE
        wide = jnp.concatenate([own_scores[h], dscores[h]], axis=0)
        outs.append((dot(stack_sources((ks, ki, ko), h), wide, TN) * SCALE).astype(bf16))
    for h, out in enumerate(outs):
        for e in range(group):
            lanes = slice((h * group + e) * HEAD_DIM, (h * group + e + 1) * HEAD_DIM)
            dq[:, lanes] = out[:, e * HEAD_DIM : (e + 1) * HEAD_DIM].T


def add_kernel(a, b, c, out):
    out[...] = (a[...] + b[...].astype(jnp.float32) + c[...].astype(jnp.float32)).astype(out.dtype)


def last_kernel(values, a, b, c, dv, dk):
    add_kernel(a, b, c, dk)
    dv[...] = values[...]


def shards(queries, keys, values, grad_out, stretch_order, block_keep):
    span = keys.shape[0]
    width = keys.shape[1]
    kv_heads = width // HEAD_DIM
    group = queries.shape[1] // width

    f32, bf16 = jnp.float32, jnp.bfloat16
    vmem = pl.BlockSpec(memory_space=pltpu.VMEM)
    hbm = pl.BlockSpec(memory_space=pltpu.HBM)
    rows = jax.ShapeDtypeStruct(queries.shape, bf16)
    wide = group * HEAD_DIM
    away = jax.ShapeDtypeStruct((kv_heads, 2 * span, wide), bf16)
    own16 = jax.ShapeDtypeStruct((kv_heads, span, wide), bf16)
    own32 = jax.ShapeDtypeStruct((kv_heads, span, wide), f32)
    stat = jax.ShapeDtypeStruct((kv_heads, 8, wide), f32)
    kv32 = jax.ShapeDtypeStruct((span, width), f32)
    kv16 = jax.ShapeDtypeStruct((span, width), bf16)
    work = [pltpu.VMEM(away.shape, bf16), pltpu.VMEM(stat.shape, f32)]

    def call(kernel, ins, out_shape, scratch=()):
        return pl.pallas_call(
            kernel,
            in_specs=ins,
            out_specs=[vmem] * len(out_shape),
            out_shape=out_shape,
            scratch_shapes=scratch,
            compiler_params=pltpu.CompilerParams(vmem_limit_bytes=VMEM),
            cost_estimate=pl.CostEstimate(flops=1, bytes_accessed=1, transcendentals=0),
        )

    def run(kernel, ins, out_shape, scratch=()):
        return call(functools.partial(kernel, group), [vmem] * len(ins), out_shape, scratch)(*ins)

    k_out = ring(keys, "outer", 1)
    k_in = ring(keys, "inner", 1)
    tables = stretch_order.T, block_keep.transpose(1, 2, 3, 0)
    q, g, k, v, bias = call(
        stage_kernel,
        [hbm] * 6,
        [rows, rows, kv16, kv16, jax.ShapeDtypeStruct((3 * span, span), f32)],
        [pltpu.VMEM(x.shape, x.dtype) for x in tables] + [pltpu.SemaphoreType.DMA((6,))],
    )(*(pltpu.with_memory_space_constraint(x, pltpu.HBM) for x in (*tables, queries, grad_out, keys, values)))
    v_out = ring(v, "outer", 1)
    v_in = ring(v, "inner", 1)
    raised, grad_probs, stats = run(own_kernel, (bias, q, g, k, v), [own16, own32, stat])
    outer_raised, outer_stats = run(
        outer_kernel, (bias, q, k_out), [own16, stat], [pltpu.VMEM(own16.shape, bf16), pltpu.VMEM(stat.shape, f32)]
    )
    probs, row_scale, dvo, dvi = run(
        probs_kernel, (bias, q, g, k_in, stats, outer_raised, outer_stats), [away, stat, kv16, kv16], work
    )
    dv_in = ring(dvi, "inner", -1)
    dv_out = ring(dvo, "outer", -1)
    dscores, deltas, dko, dki = run(
        scores_kernel, (q, g, v_in, v_out, probs, row_scale), [away, stat, kv16, kv16], work
    )
    dk_in = ring(dki, "inner", -1)
    dk_out = ring(dko, "outer", -1)
    dq, dks, dvs = run(
        queries_kernel,
        (q, g, k, k_in, k_out, raised, grad_probs, row_scale, deltas, dscores),
        [rows, kv32, kv32],
        [pltpu.VMEM(own16.shape, bf16)] * 2,
    )
    (dv,) = call(add_kernel, [vmem] * 3, [kv16])(dvs, dv_out, dv_in)
    dv, dk = call(last_kernel, [vmem] * 4, [kv16, kv16])(dv, dks, dk_in, dk_out)
    return dq, dk, dv


def solution(mesh):
    rows = P(("outer", "inner"), None)
    return jax.shard_map(
        shards, mesh=mesh, in_specs=(rows, rows, rows, rows, P(), P()), out_specs=(rows, rows, rows), check_vma=False
    )
```
